32 devices in a mesh: doc: 8 (over z, y), feat: 4 (over x, core).
Axes of the slice: x: 2, y: 2, z: 4, core: 2. Of those that a mesh axis runs over, the one named last changes fastest.
Arguments:
- scores: float32 [96, 128], P('doc'), may hold values from -6 to 6
- clicks: int32 [96, 128], P('doc'), may hold values from 0 to 1, as said below
- lengths: int32 [96], P('doc'), may hold values from 2 to 128, as said below
- t_plus_old: float32 [128], replicated, may hold values from 0.1 to 1
- t_minus_old: float32 [128], replicated, may hold values from 0.1 to 1
- leaf: int32 [12288], P('doc'), may hold values from 0 to 31
- bins: int32 [512, 12288], P('feat', 'doc'), may hold values from 0 to 255
Outputs:
- t_plus: float32 [128], replicated
- t_minus: float32 [128], replicated
- gradients: float32 [2, 12288], P(None, 'doc')
- hist: float32 [512, 64, 256], P(('feat', 'doc'))
The draws below stay inside these ranges and needn't reach their ends.
Inputs may be any that keep to these rules, and one draw needn't show every extreme that they name: Query q shows its first lengths[q] slots; the first two queries of each block of 12 queries show all 128. `clicks`: values at or beyond a query's length carry no meaning. In the first query of each block of 12 queries the even positions are clicked and the odd ones not; in the second the reverse.
All inputs are finite; a program needn't handle non-finite values.
Results may differ from the reference program's by a relative error of at most 0.0024.
Values may be sent and summed in bfloat16 or wider, within the bound.
A program may use at most 64 MiB of HBM per device.

```python
import math
import jax
import jax.numpy as jnp
from jax import lax

POS = 128
F = 512
BINS = 256
LEAVES = 32
Q_DEV = 12
QUERIES = 96
DOCS = 12288


def shared_layout(key):
    key_size = jax.random.fold_in(key, 11)
    key_click = jax.random.fold_in(key, 12)
    query_index = jnp.arange(QUERIES, dtype=jnp.int32)
    inside = query_index % Q_DEV
    drawn_count = jax.random.randint(key_size, (QUERIES,), 2, POS + 1, dtype=jnp.int32)
    drawn_count = jnp.where(inside < 2, POS, drawn_count).astype(jnp.int32)
    places = jnp.arange(POS, dtype=jnp.int32)
    whole = QUERIES * POS
    reach = whole - jnp.minimum(whole, 2 * places[None, :] * query_index[:, None])
    permille = 50 + 350 * reach // whole
    draws = jax.random.randint(key_click, (QUERIES, POS), 0, 1000, dtype=jnp.int32)
    labels = jnp.where(draws < permille, 1, 0)
    even_mark = jnp.where(places % 2 == 0, 1, 0)
    labels = jnp.where((inside == 0)[:, None], even_mark[None, :], labels)
    labels = jnp.where((inside == 1)[:, None], 1 - even_mark[None, :], labels)
    return (drawn_count, labels.astype(jnp.int32))


def draw_lengths(key, part):
    return shared_layout(key)[0]


def draw_clicks(key, part):
    return shared_layout(key)[1]


def touch_ends(values, own_key, least, top_value):
    extent = values.shape
    spot = [jax.random.randint(jax.random.fold_in(own_key, axis), (), 0, extent[axis]) for axis in range(len(extent))]
    values = values.at[tuple(spot)].set(least)
    longest = extent.index(max(extent))
    spot[longest] = (spot[longest] + 1) % extent[longest]
    return values.at[tuple(spot)].set(top_value)


def steps_of(key, dims, pieces, low, largest):
    gain, own = 1.0, jax.random.fold_in(key, 6)
    for axis_at, shards_of in pieces:
        heights = jnp.exp(jax.random.uniform(jax.random.fold_in(own, axis_at), (shards_of,), jnp.float32, low / len(pieces), largest / len(pieces)))
        gain = gain * jnp.repeat(heights, dims[axis_at] // shards_of).reshape([-1 if axis == axis_at else 1 for axis in range(len(dims))])
    return gain


def centred(rng, shape, width, most, pieces=(), kind=jnp.bfloat16):
    array = jax.random.normal(rng, shape, jnp.float32) * width
    if len(pieces) > 0:
        array = steps_of(rng, shape, pieces, -0.22, 0.18) * array
    return jnp.clip(array, min=-most, max=most).astype(kind)


def setup_inputs(seed: int = 0) -> dict:
    seeds = jax.random.split(jax.random.key(seed), 8)
    return {
        "scores": centred(seeds[0], (QUERIES, POS), 1.0, 6.0, ((0, 8),), jnp.float32),
        "clicks": draw_clicks(jax.random.fold_in(seeds[7], 71), 0),
        "lengths": draw_lengths(jax.random.fold_in(seeds[7], 71), 0),
        "t_plus_old": jnp.clip(jnp.exp(jax.random.uniform(seeds[3], (POS,), jnp.float32, math.log(0.1), math.log(1.0))), 0.1, 1.0),
        "t_minus_old": jnp.clip(jnp.exp(jax.random.uniform(seeds[4], (POS,), jnp.float32, math.log(0.1), math.log(1.0))), 0.1, 1.0),
        "leaf": touch_ends(jax.random.randint(seeds[5], (DOCS,), 0, LEAVES), jax.random.fold_in(seeds[5], 1), 0, LEAVES - 1).astype(jnp.int32),
        "bins": touch_ends(jax.random.randint(seeds[6], (F, DOCS), 0, BINS), jax.random.fold_in(seeds[6], 1), 0, BINS - 1).astype(jnp.int32),
    }


def pair_terms(scores, clicks, lengths, t_plus_old, t_minus_old):
    npos = scores.shape[1]
    places = jnp.arange(npos)
    shown_mask = places[None, :] < lengths[:, None]
    clicked = jnp.where((clicks == 1) & shown_mask, 1.0, 0.0).astype(jnp.float32)
    skipped = jnp.where((clicks == 0) & shown_mask, 1.0, 0.0).astype(jnp.float32)
    paired = clicked[:, :, None] * skipped[:, None, :]
    discount = 1.0 / jnp.log2(2.0 + places.astype(jnp.float32))
    clicks_count = lax.optimization_barrier(jnp.sum(clicked, axis=1))
    ideal_gain = lax.optimization_barrier(jnp.sum(jnp.where(places[None, :].astype(jnp.float32) < clicks_count[:, None], discount[None, :], 0.0), axis=1))
    ideal_gain = jnp.maximum(ideal_gain, 1.0)
    change = paired * jnp.abs(discount[:, None] - discount[None, :])[None] / ideal_gain[:, None, None]
    spread = scores[:, :, None] - scores[:, None, :]
    weighted = change * jax.nn.softplus(-spread)
    plus_part = lax.optimization_barrier(jnp.sum(weighted / t_minus_old[None, None, :], axis=(0, 2)))
    minus_part = lax.optimization_barrier(jnp.sum(weighted / t_plus_old[None, :, None], axis=(0, 1)))
    return (change, spread, plus_part, minus_part)

def lambda_terms(change, spread, t_plus, t_minus):
    scaled = change / (t_plus[None, :, None] * t_minus[None, None, :])
    chance = jax.nn.sigmoid(-spread)
    lambda_pair = scaled * chance
    second = lambda_pair * (1.0 - chance)
    slopes = lax.optimization_barrier(jnp.sum(lambda_pair, axis=1)) - lax.optimization_barrier(jnp.sum(lambda_pair, axis=2))
    curvature = lax.optimization_barrier(jnp.sum(second, axis=1)) + lax.optimization_barrier(jnp.sum(second, axis=2))
    return (slopes, curvature)

def reference(scores, clicks, lengths, t_plus_old, t_minus_old, leaf, bins):
    change, spread, plus_sum, minus_sum = pair_terms(scores, clicks, lengths, t_plus_old, t_minus_old)
    t_plus = jnp.sqrt(plus_sum / plus_sum[0])
    t_minus = jnp.sqrt(minus_sum / minus_sum[0])
    slopes, curvature = lambda_terms(change, spread, t_plus, t_minus)
    gradients = jnp.stack([slopes.reshape(-1), curvature.reshape(-1)])
    rounded = lax.optimization_barrier(gradients.astype(jnp.bfloat16)).astype(jnp.float32)
    values = jnp.transpose(rounded)

    def one_feature(column):
        segment_ids = leaf * BINS + column
        summed = jax.ops.segment_sum(values, segment_ids, num_segments=LEAVES * BINS)
        summed = summed.reshape(LEAVES, BINS, 2)
        return jnp.transpose(summed, (2, 0, 1)).reshape(2 * LEAVES, BINS)
    hist = lax.map(one_feature, bins)
    return (t_plus, t_minus, gradients, hist)
```

```python
import functools

import jax
import jax.numpy as jnp
from jax import lax
from jax.experimental import pallas as pl
from jax.experimental.pallas import tpu as pltpu
from jax.sharding import PartitionSpec as P

BINS = 256
LEAVES = 32
F8 = jnp.float8_e4m3fn
BF = jnp.bfloat16
F32 = jnp.float32
MESH = pl.DeviceIdType.MESH
NT = (((1,), (1,)), ((), ()))


def rows_kernel(
    ndoc,
    scores_ref,
    clicks_ref,
    lengths_ref,
    tpo_ref,
    tmo_ref,
    leaf_ref,
    bins_ref,
    tp_ref,
    tm_ref,
    grad_ref,
    cols_ref,
    pk_ref,
    bins_bf,
    sums,
    turn,
    pair_g,
    pair_h,
    send_sem,
    recv_sem,
):
    nq, npos = scores_ref.shape
    me = lax.axis_index("doc")
    peers = [lax.rem(me + o, ndoc) for o in range(ndoc)]
    barrier = pltpu.get_barrier_semaphore()
    for o in range(1, ndoc):
        pl.semaphore_signal(barrier, inc=1, device_id={"doc": peers[o]}, device_id_type=MESH)

    def send(kind, o, src, dst):
        return pltpu.make_async_remote_copy(
            src_ref=src,
            dst_ref=dst,
            send_sem=send_sem.at[kind, o],
            recv_sem=recv_sem.at[kind, o],
            device_id={"doc": peers[o]},
            device_id_type=MESH,
        )

    def cast(p, carry):
        bins_bf[p] = bins_ref[p].astype(F32).astype(BF)
        return carry

    lax.fori_loop(0, ndoc, cast, 0)
    pl.semaphore_wait(barrier, ndoc - 1)
    col_copies = [send(0, o, bins_bf.at[peers[o]], cols_ref.at[me]) for o in range(1, ndoc)]
    for copy in col_copies:
        copy.start()
    cols_ref[me] = bins_bf[me]

    place = lax.broadcasted_iota(jnp.int32, (nq, npos), 1)
    shown = place < lengths_ref[...]
    clicked = jnp.logical_and(shown, clicks_ref[...] == 1)
    skipped = jnp.logical_and(shown, clicks_ref[...] == 0)
    code = jnp.where(clicked, 1.0, jnp.where(skipped, -1.0, 0.0)).astype(F32)
    count = jnp.sum(jnp.where(clicked, 1.0, 0.0), axis=1, keepdims=True)
    to_log2 = 1.4426950408889634
    disc_row = 1.0 / (jnp.log(2.0 + lax.broadcasted_iota(jnp.int32, (8, npos), 1).astype(F32)) * to_log2)
    disc_row = disc_row[0:1]
    ideal = jnp.sum(jnp.where(place.astype(F32) < count, disc_row, 0.0), axis=1, keepdims=True)
    gain = 1.0 / jnp.maximum(ideal, 1.0)
    weigh = jnp.where(clicked, 1.0 / tpo_ref[...], 1.0 / tmo_ref[...])
    turn[...] = jnp.zeros_like(turn)
    turn[0:nq] = scores_ref[...]
    turn[16 : 16 + nq] = code
    turn[32 : 32 + nq] = weigh
    turn[48:49] = disc_row
    stood = turn[...].T
    gap = jnp.abs(stood[:, 48:49] - disc_row)
    plus_row = jnp.zeros((1, npos), F32)
    minus_row = jnp.zeros((1, npos), F32)
    for q in range(nq):
        code_col = stood[:, 16 + q : 17 + q]
        code_row = code[q : q + 1]
        away = jnp.where(code_col * code_row < 0.0, gap, 0.0)
        y = code_col * (scores_ref[q : q + 1, :] - stood[:, q : q + 1])
        e = jnp.exp(-jnp.abs(y))
        inv = 1.0 / (1.0 + e)
        small = e * (1.0 - e * (0.5 - e * (1.0 / 3.0)))
        soft = jnp.maximum(y, 0.0) + jnp.where(e < 0.01, small, jnp.log(1.0 + e))
        loss = jnp.sum(away * soft * stood[:, 32 + q : 33 + q], axis=0, keepdims=True)
        loss = loss * gain[q : q + 1]
        plus_row = plus_row + jnp.where(code_row > 0.0, loss, 0.0)
        minus_row = minus_row + jnp.where(code_row < 0.0, loss, 0.0)
        scaled = away * inv
        pair_g[q] = code_col * scaled * jnp.where(y >= 0.0, 1.0, e)
        pair_h[q] = scaled * inv * e
    sums[me, 0:1] = plus_row
    sums[me, 1:2] = minus_row
    sum_copies = [send(1, o, sums.at[me], sums.at[me]) for o in range(1, ndoc)]
    for copy in sum_copies:
        copy.start()
    for copy in sum_copies:
        copy.wait()
    total = jnp.sum(sums[...], axis=0)
    t_new = jnp.sqrt(total / total[:, 0:1])
    tp_ref[...] = t_new[0:1]
    tm_ref[...] = t_new[1:2]
    t_inv = 1.0 / t_new
    unit = jnp.where(clicked, t_inv[0:1], t_inv[1:2])
    turn[0:nq] = unit
    unit_col = turn[...].T
    unit_row = unit * gain
    for q in range(nq):
        lanes = slice(q * npos, (q + 1) * npos)
        side = unit_col[:, q : q + 1]
        slope = jnp.sum(pair_g[q] * side, axis=0, keepdims=True) * unit_row[q : q + 1]
        curve = jnp.sum(pair_h[q] * side, axis=0, keepdims=True) * unit_row[q : q + 1]
        both = jnp.concatenate([slope, curve], axis=0)
        grad_ref[:, lanes] = both
        leaf_row = leaf_ref[:, lanes].astype(F32)
        pk_ref[me, :, lanes] = jnp.concatenate([both, leaf_row], axis=0).astype(BF)
    pk_copies = [send(2, o, pk_ref.at[me], pk_ref.at[me]) for o in range(1, ndoc)]
    for copy in pk_copies:
        copy.start()
    for copy in pk_copies + col_copies:
        copy.wait()


def hist_kernel(cols_ref, pk_ref, out_ref, w_ref, scale_ref):
    step = pl.program_id(0)
    nfeat, rows = cols_ref.shape[1], cols_ref.shape[2]

    @pl.when(step == 0)
    def _():
        out_ref[...] = jnp.zeros_like(out_ref)
        top = jnp.max(jnp.abs(pk_ref[:, 0:2, :].astype(F32)), axis=0)
        top = jnp.maximum(jnp.max(top, axis=1, keepdims=True), 1e-30)
        power = jnp.clip(jnp.floor(jnp.log(top) * 1.4426950408889634), -110.0, 110.0).astype(jnp.int32)
        power = jnp.broadcast_to(power, (2, 128))
        size, tiny = jnp.abs(power), power < 0
        up = jnp.full((2, 128), 128.0, F32)
        down = jnp.full((2, 128), 1.0 / 128.0, F32)
        for bit in range(7):
            on = ((size >> bit) & 1) == 1
            large, less = F32(2.0 ** (2**bit)), F32(2.0 ** -(2**bit))
            up = up * jnp.where(on, jnp.where(tiny, large, less), F32(1.0))
            down = down * jnp.where(on, jnp.where(tiny, less, large), F32(1.0))
        scale_ref[0:2] = up
        scale_ref[2:4] = down

    pack = pk_ref[step]
    leaf = pack[2:3]
    value = (pack[0:2].astype(F32) * scale_ref[0:2, 0:1]).astype(BF)
    high = value.astype(F8).astype(BF)
    low = (value - high) * BF(16.0)
    levels = lax.broadcasted_iota(jnp.int32, (LEAVES, rows), 0).astype(BF)
    hit = levels == leaf
    none = jnp.zeros((), BF)
    w_ref[...] = jnp.concatenate(
        [jnp.where(hit, part, none) for part in (high[0:1], high[1:2], low[0:1], low[1:2])], axis=0
    ).astype(F8)
    bins = lax.broadcasted_iota(jnp.int32, (BINS, rows), 0).astype(BF)
    for f in range(nfeat):
        one_hot = jnp.where(cols_ref[0, f : f + 1, :] == bins, jnp.ones((), BF), none).astype(F8)
        got = lax.dot_general(w_ref[...], one_hot, NT, preferred_element_type=F32)
        out_ref[f] += got[: 2 * LEAVES] + got[2 * LEAVES :] * (1.0 / 16.0)

    @pl.when(step == pl.num_programs(0) - 1)
    def _():
        for f in range(nfeat):
            out_ref[f, :LEAVES] *= scale_ref[2:3, 0:1]
            out_ref[f, LEAVES:] *= scale_ref[3:4, 0:1]


def body(scores, clicks, lengths, t_plus_old, t_minus_old, leaf, bins):
    ndoc = lax.axis_size("doc")
    nq, npos = scores.shape
    rows = leaf.shape[0]
    nfeat = bins.shape[0] // ndoc
    vmem = pl.BlockSpec(memory_space=pltpu.VMEM)
    t_plus, t_minus, gradients, cols, packs = pl.pallas_call(
        functools.partial(rows_kernel, ndoc),
        out_shape=(
            jax.ShapeDtypeStruct((1, npos), F32),
            jax.ShapeDtypeStruct((1, npos), F32),
            jax.ShapeDtypeStruct((2, rows), F32),
            jax.ShapeDtypeStruct((ndoc, nfeat, rows), BF),
            jax.ShapeDtypeStruct((ndoc, 3, rows), BF),
        ),
        in_specs=[vmem] * 7,
        out_specs=(vmem,) * 5,
        scratch_shapes=[
            pltpu.VMEM((ndoc, nfeat, rows), BF),
            pltpu.VMEM((ndoc, 2, npos), F32),
            pltpu.VMEM((npos, npos), F32),
            pltpu.VMEM((nq, npos, npos), F32),
            pltpu.VMEM((nq, npos, npos), F32),
            pltpu.SemaphoreType.DMA((3, ndoc)),
            pltpu.SemaphoreType.DMA((3, ndoc)),
        ],
        compiler_params=pltpu.CompilerParams(
            collective_id=0, has_side_effects=True, vmem_limit_bytes=40 << 20
        ),
    )(
        scores,
        clicks,
        lengths.reshape(nq, 1),
        t_plus_old.reshape(1, npos),
        t_minus_old.reshape(1, npos),
        leaf.reshape(1, rows),
        bins.reshape(ndoc, nfeat, rows),
    )
    hist = pl.pallas_call(
        hist_kernel,
        grid=(ndoc,),
        out_shape=jax.ShapeDtypeStruct((nfeat, 2 * LEAVES, BINS), F32),
        in_specs=[
            pl.BlockSpec((1, nfeat, rows), lambda i: (i, 0, 0)),
            pl.BlockSpec((ndoc, 3, rows), lambda i: (0, 0, 0)),
        ],
        out_specs=pl.BlockSpec((nfeat, 2 * LEAVES, BINS), lambda i: (0, 0, 0)),
        scratch_shapes=[pltpu.VMEM((4 * LEAVES, rows), F8), pltpu.VMEM((4, 128), F32)],
        compiler_params=pltpu.CompilerParams(vmem_limit_bytes=40 << 20),
    )(cols, packs)
    return (t_plus.reshape(npos), t_minus.reshape(npos), gradients, hist)


def solution(mesh):
    placed = (P("doc", None), P("doc", None), P("doc"), P(), P(), P("doc"), P("feat", "doc"))
    return jax.shard_map(
        body,
        mesh=mesh,
        in_specs=placed,
        out_specs=(P(), P(), P(None, "doc"), P(("feat", "doc"), None, None)),
        check_vma=False,
    )
```

```python
import functools

import jax
import jax.numpy as jnp
from jax import lax
from jax.experimental import pallas as pl
from jax.experimental.pallas import tpu as pltpu
from jax.sharding import PartitionSpec as P

BINS = 256
LEAVES = 32
F8 = jnp.float8_e4m3fn
BF = jnp.bfloat16
F32 = jnp.float32
MESH = pl.DeviceIdType.MESH
NT = (((1,), (1,)), ((), ()))


def rows_kernel(
    ndoc,
    scores_in,
    clicks_in,
    lengths_ref,
    tpo_in,
    tmo_in,
    leaf_in,
    bins_in,
    tp_ref,
    tm_ref,
    grad_ref,
    cols_ref,
    pk_ref,
    bins_bf,
    sums,
    turn,
    pair_g,
    pair_h,
    scores_ref,
    clicks_ref,
    tpo_ref,
    tmo_ref,
    leaf_ref,
    bins_ref,
    send_sem,
    recv_sem,
    in_sem,
):
    nq, npos = scores_ref.shape
    bins_load = pltpu.make_async_copy(bins_in, bins_ref, in_sem.at[0])
    bins_load.start()
    pairs = [
        (scores_in, scores_ref),
        (clicks_in, clicks_ref),
        (tpo_in, tpo_ref),
        (tmo_in, tmo_ref),
        (leaf_in, leaf_ref),
    ]
    loads = [pltpu.make_async_copy(a, b, in_sem.at[1 + k]) for k, (a, b) in enumerate(pairs)]
    for load in loads:
        load.start()
    me = lax.axis_index("doc")
    peers = [lax.rem(me + o, ndoc) for o in range(ndoc)]
    barrier = pltpu.get_barrier_semaphore()
    for o in range(1, ndoc):
        pl.semaphore_signal(barrier, inc=1, device_id={"doc": peers[o]}, device_id_type=MESH)

    def send(kind, o, src, dst):
        return pltpu.make_async_remote_copy(
            src_ref=src,
            dst_ref=dst,
            send_sem=send_sem.at[kind, o],
            recv_sem=recv_sem.at[kind, o],
            device_id={"doc": peers[o]},
            device_id_type=MESH,
        )

    def cast(p, carry):
        bins_bf[p] = bins_ref[p].astype(F32).astype(BF)
        return carry

    bins_load.wait()
    lax.fori_loop(0, ndoc, cast, 0)
    pl.semaphore_wait(barrier, ndoc - 1)
    col_copies = [send(0, o, bins_bf.at[peers[o]], cols_ref.at[me]) for o in range(1, ndoc)]
    for copy in col_copies:
        copy.start()
    cols_ref[me] = bins_bf[me]

    for load in loads:
        load.wait()
    place = lax.broadcasted_iota(jnp.int32, (nq, npos), 1)
    shown = place < lengths_ref[...]
    clicked = jnp.logical_and(shown, clicks_ref[...] == 1)
    skipped = jnp.logical_and(shown, clicks_ref[...] == 0)
    code = jnp.where(clicked, 1.0, jnp.where(skipped, -1.0, 0.0)).astype(F32)
    count = jnp.sum(jnp.where(clicked, 1.0, 0.0), axis=1, keepdims=True)
    to_log2 = 1.4426950408889634
    disc_row = 1.0 / (jnp.log(2.0 + lax.broadcasted_iota(jnp.int32, (8, npos), 1).astype(F32)) * to_log2)
    disc_row = disc_row[0:1]
    ideal = jnp.sum(jnp.where(place.astype(F32) < count, disc_row, 0.0), axis=1, keepdims=True)
    gain = 1.0 / jnp.maximum(ideal, 1.0)
    weigh = jnp.where(clicked, 1.0 / tpo_ref[...], 1.0 / tmo_ref[...])
    turn[...] = jnp.zeros_like(turn)
    turn[0:nq] = scores_ref[...]
    turn[16 : 16 + nq] = code
    turn[32 : 32 + nq] = weigh
    turn[48:49] = disc_row
    stood = turn[...].T
    gap = jnp.abs(stood[:, 48:49] - disc_row)
    plus_row = jnp.zeros((1, npos), F32)
    minus_row = jnp.zeros((1, npos), F32)
    for q in range(nq):
        code_col = stood[:, 16 + q : 17 + q]
        code_row = code[q : q + 1]
        away = jnp.where(code_col * code_row < 0.0, gap, 0.0)
        y = code_col * (scores_ref[q : q + 1, :] - stood[:, q : q + 1])
        e = jnp.exp(-jnp.abs(y))
        inv = 1.0 / (1.0 + e)
        small = e * (1.0 - e * (0.5 - e * (1.0 / 3.0)))
        soft = jnp.maximum(y, 0.0) + jnp.where(e < 0.01, small, jnp.log(1.0 + e))
        loss = jnp.sum(away * soft * stood[:, 32 + q : 33 + q], axis=0, keepdims=True)
        loss = loss * gain[q : q + 1]
        plus_row = plus_row + jnp.where(code_row > 0.0, loss, 0.0)
        minus_row = minus_row + jnp.where(code_row < 0.0, loss, 0.0)
        scaled = away * inv
        pair_g[q] = code_col * scaled * jnp.where(y >= 0.0, 1.0, e)
        pair_h[q] = scaled * inv * e
    sums[me, 0:1] = plus_row
    sums[me, 1:2] = minus_row
    sum_copies = [send(1, o, sums.at[me], sums.at[me]) for o in range(1, ndoc)]
    for copy in sum_copies:
        copy.start()
    for copy in sum_copies:
        copy.wait()
    total = jnp.sum(sums[...], axis=0)
    t_new = jnp.sqrt(total / total[:, 0:1])
    tp_ref[...] = t_new[0:1]
    tm_ref[...] = t_new[1:2]
    t_inv = 1.0 / t_new
    unit = jnp.where(clicked, t_inv[0:1], t_inv[1:2])
    turn[0:nq] = unit
    unit_col = turn[...].T
    unit_row = unit * gain
    for q in range(nq):
        lanes = slice(q * npos, (q + 1) * npos)
        side = unit_col[:, q : q + 1]
        slope = jnp.sum(pair_g[q] * side, axis=0, keepdims=True) * unit_row[q : q + 1]
        curve = jnp.sum(pair_h[q] * side, axis=0, keepdims=True) * unit_row[q : q + 1]
        both = jnp.concatenate([slope, curve], axis=0)
        grad_ref[:, lanes] = both
        leaf_row = leaf_ref[lanes].astype(F32).reshape(1, npos)
        pk_ref[me, :, lanes] = jnp.concatenate([both, leaf_row], axis=0).astype(BF)
    pk_copies = [send(2, o, pk_ref.at[me], pk_ref.at[me]) for o in range(1, ndoc)]
    for copy in pk_copies:
        copy.start()
    for copy in pk_copies + col_copies:
        copy.wait()


def hist_kernel(
    cols_ref, pk_ref, tp_in, tm_in, grad_in, out_ref, tp_ref, tm_ref, grad_ref, w_ref, scale_ref
):
    step = pl.program_id(0)
    nfeat, rows = cols_ref.shape[1], cols_ref.shape[2]

    @pl.when(step == 0)
    def _():
        out_ref[...] = jnp.zeros_like(out_ref)
        tp_ref[...] = tp_in[...]
        tm_ref[...] = tm_in[...]
        grad_ref[...] = grad_in[...]
        top = jnp.max(jnp.abs(pk_ref[:, 0:2, :].astype(F32)), axis=0)
        top = jnp.maximum(jnp.max(top, axis=1, keepdims=True), 1e-30)
        power = jnp.clip(jnp.floor(jnp.log(top) * 1.4426950408889634), -110.0, 110.0).astype(jnp.int32)
        power = jnp.broadcast_to(power, (2, 128))
        size, tiny = jnp.abs(power), power < 0
        up = jnp.full((2, 128), 128.0, F32)
        down = jnp.full((2, 128), 1.0 / 128.0, F32)
        for bit in range(7):
            on = ((size >> bit) & 1) == 1
            large, less = F32(2.0 ** (2**bit)), F32(2.0 ** -(2**bit))
            up = up * jnp.where(on, jnp.where(tiny, large, less), F32(1.0))
            down = down * jnp.where(on, jnp.where(tiny, less, large), F32(1.0))
        scale_ref[0:2] = up
        scale_ref[2:4] = down

    pack = pk_ref[step]
    leaf = pack[2:3]
    value = (pack[0:2].astype(F32) * scale_ref[0:2, 0:1]).astype(BF)
    high = value.astype(F8).astype(BF)
    low = (value - high) * BF(16.0)
    levels = lax.broadcasted_iota(jnp.int32, (LEAVES, rows), 0).astype(BF)
    hit = levels == leaf
    none = jnp.zeros((), BF)
    w_ref[...] = jnp.concatenate(
        [jnp.where(hit, part, none) for part in (high[0:1], high[1:2], low[0:1], low[1:2])], axis=0
    ).astype(F8)
    bins = lax.broadcasted_iota(jnp.int32, (BINS, rows), 0).astype(BF)
    for f in range(nfeat):
        one_hot = jnp.where(cols_ref[0, f : f + 1, :] == bins, jnp.ones((), BF), none).astype(F8)
        got = lax.dot_general(w_ref[...], one_hot, NT, preferred_element_type=F32)
        out_ref[f] += got[: 2 * LEAVES] + got[2 * LEAVES :] * (1.0 / 16.0)

    @pl.when(step == pl.num_programs(0) - 1)
    def _():
        for f in range(nfeat):
            out_ref[f, :LEAVES] *= scale_ref[2:3, 0:1]
            out_ref[f, LEAVES:] *= scale_ref[3:4, 0:1]


def body(scores, clicks, lengths, t_plus_old, t_minus_old, leaf, bins):
    ndoc = lax.axis_size("doc")
    nq, npos = scores.shape
    rows = leaf.shape[0]
    nfeat = bins.shape[0] // ndoc
    anyw = pl.BlockSpec(memory_space=pltpu.HBM)
    vmem = pl.BlockSpec(memory_space=pltpu.VMEM)
    t_plus, t_minus, gradients, cols, packs = pl.pallas_call(
        functools.partial(rows_kernel, ndoc),
        out_shape=(
            jax.ShapeDtypeStruct((1, npos), F32),
            jax.ShapeDtypeStruct((1, npos), F32),
            jax.ShapeDtypeStruct((2, rows), F32),
            jax.ShapeDtypeStruct((ndoc, nfeat, rows), BF),
            jax.ShapeDtypeStruct((ndoc, 3, rows), BF),
        ),
        in_specs=[anyw, anyw, vmem, anyw, anyw, anyw, anyw],
        out_specs=(vmem,) * 5,
        scratch_shapes=[
            pltpu.VMEM((ndoc, nfeat, rows), BF),
            pltpu.VMEM((ndoc, 2, npos), F32),
            pltpu.VMEM((npos, npos), F32),
            pltpu.VMEM((nq, npos, npos), F32),
            pltpu.VMEM((nq, npos, npos), F32),
            pltpu.VMEM((nq, npos), F32),
            pltpu.VMEM((nq, npos), jnp.int32),
            pltpu.VMEM((1, npos), F32),
            pltpu.VMEM((1, npos), F32),
            pltpu.VMEM((rows,), jnp.int32),
            pltpu.VMEM((ndoc, nfeat, rows), jnp.int32),
            pltpu.SemaphoreType.DMA((3, ndoc)),
            pltpu.SemaphoreType.DMA((3, ndoc)),
            pltpu.SemaphoreType.DMA((6,)),
        ],
        compiler_params=pltpu.CompilerParams(
            collective_id=0, has_side_effects=True, vmem_limit_bytes=40 << 20
        ),
    )(
        scores,
        clicks,
        lengths.reshape(nq, 1),
        t_plus_old.reshape(1, npos),
        t_minus_old.reshape(1, npos),
        leaf,
        bins.reshape(ndoc, nfeat, rows),
    )
    whole = [pl.BlockSpec(a.shape, lambda i: (0, 0)) for a in (t_plus, t_minus, gradients)]
    hist, t_plus, t_minus, gradients = pl.pallas_call(
        hist_kernel,
        grid=(ndoc,),
        out_shape=(
            jax.ShapeDtypeStruct((nfeat, 2 * LEAVES, BINS), F32),
            jax.ShapeDtypeStruct(t_plus.shape, F32),
            jax.ShapeDtypeStruct(t_minus.shape, F32),
            jax.ShapeDtypeStruct(gradients.shape, F32),
        ),
        in_specs=[
            pl.BlockSpec((1, nfeat, rows), lambda i: (i, 0, 0)),
            pl.BlockSpec((ndoc, 3, rows), lambda i: (0, 0, 0)),
            *whole,
        ],
        out_specs=(pl.BlockSpec((nfeat, 2 * LEAVES, BINS), lambda i: (0, 0, 0)), *whole),
        scratch_shapes=[pltpu.VMEM((4 * LEAVES, rows), F8), pltpu.VMEM((4, 128), F32)],
        compiler_params=pltpu.CompilerParams(vmem_limit_bytes=40 << 20),
    )(cols, packs, t_plus, t_minus, gradients)
    return (t_plus.reshape(npos), t_minus.reshape(npos), gradients, hist)


def solution(mesh):
    placed = (P("doc", None), P("doc", None), P("doc"), P(), P(), P("doc"), P("feat", "doc"))
    return jax.shard_map(
        body,
        mesh=mesh,
        in_specs=placed,
        out_specs=(P(), P(), P(None, "doc"), P(("feat", "doc"), None, None)),
        check_vma=False,
    )
```

```python
import functools

import jax
import jax.numpy as jnp
from jax import lax
from jax.experimental import pallas as pl
from jax.experimental.pallas import tpu as pltpu
from jax.sharding import PartitionSpec as P

BINS = 256
LEAVES = 32
F8 = jnp.float8_e4m3fn
BF = jnp.bfloat16
F32 = jnp.float32
EARLY = 1
MESH = pl.DeviceIdType.MESH
NT = (((1,), (1,)), ((), ()))


def partner(me, step, ndoc):
    if ndoc & (ndoc - 1):
        return lax.rem(step - me + ndoc, ndoc)
    other = me
    bit = 1
    while bit < ndoc:
        if step & bit:
            other = other + (1 - 2 * ((me // bit) % 2)) * bit
        bit *= 2
    return other


def power_scale(top, width):
    power = jnp.floor(jnp.log(jnp.maximum(top, 1e-30)) * 1.4426950408889634)
    power = jnp.broadcast_to(jnp.clip(power, -110.0, 110.0).astype(jnp.int32), (1, width))
    size, tiny = jnp.abs(power), power < 0
    up = jnp.full((1, width), 128.0, F32)
    down = jnp.full((1, width), 1.0 / 128.0, F32)
    for bit in range(7):
        on = ((size >> bit) & 1) == 1
        large, less = F32(2.0 ** (2**bit)), F32(2.0 ** -(2**bit))
        up = up * jnp.where(on, jnp.where(tiny, large, less), F32(1.0))
        down = down * jnp.where(on, jnp.where(tiny, less, large), F32(1.0))
    return up, down


def add_block(columns, pack, out_ref, w_ref):
    nfeat, rows = out_ref.shape[0], pack.shape[1]
    value, leaf = pack[0:2], pack[2:3]
    high = value.astype(F8).astype(BF)
    low = (value - high) * BF(16.0)
    levels = lax.broadcasted_iota(jnp.int32, (LEAVES, rows), 0).astype(BF)
    hit = levels == leaf
    none = jnp.zeros((), BF)
    w_ref[...] = jnp.concatenate(
        [jnp.where(hit, part, none) for part in (high[0:1], high[1:2], low[0:1], low[1:2])], axis=0
    ).astype(F8)
    half_row = rows // 2
    back = pack[3:4].astype(F32)
    back = jnp.concatenate(
        [
            jnp.broadcast_to(back[:, 0:1], (LEAVES, 1)),
            jnp.broadcast_to(back[:, half_row : half_row + 1], (LEAVES, 1)),
        ],
        axis=0,
    )
    bins = lax.broadcasted_iota(jnp.int32, (BINS, rows), 0).astype(BF)
    for f in range(nfeat):
        one_hot = jnp.where(columns(f) == bins, jnp.ones((), BF), none).astype(F8)
        got = lax.dot_general(w_ref[...], one_hot, NT, preferred_element_type=F32)
        out_ref[f] += (got[: 2 * LEAVES] + got[2 * LEAVES :] * (1.0 / 16.0)) * back


def rows_kernel(
    ndoc,
    scores_in,
    clicks_in,
    lengths_ref,
    tpo_in,
    tmo_in,
    leaf_in,
    bins_in,
    tp_ref,
    tm_ref,
    grad_ref,
    cols_ref,
    pk_ref,
    acc_ref,
    w_ref,
    bins_bf,
    sums,
    turn,
    pair_g,
    pair_h,
    scores_ref,
    clicks_ref,
    tpo_ref,
    tmo_ref,
    leaf_ref,
    bins_ref,
    send_sem,
    recv_sem,
    in_sem,
):
    nq, npos = scores_ref.shape
    bins_load = pltpu.make_async_copy(bins_in, bins_ref, in_sem.at[0])
    bins_load.start()
    pairs = [
        (scores_in, scores_ref),
        (clicks_in, clicks_ref),
        (tpo_in, tpo_ref),
        (tmo_in, tmo_ref),
        (leaf_in, leaf_ref),
    ]
    loads = [pltpu.make_async_copy(a, b, in_sem.at[1 + k]) for k, (a, b) in enumerate(pairs)]
    for load in loads:
        load.start()
    me = lax.axis_index("doc")
    half = max(ndoc // 2, 1)
    peers = [partner(me, o, ndoc) for o in range(ndoc)]
    barrier = pltpu.get_barrier_semaphore()
    for o in range(1, ndoc):
        pl.semaphore_signal(barrier, inc=1, device_id={"doc": peers[o]}, device_id_type=MESH)

    def send_any(kind, o, src, dst, peer=peers[-1]):
        return pltpu.make_async_remote_copy(
            src_ref=src,
            dst_ref=dst,
            send_sem=send_sem.at[kind, o],
            recv_sem=recv_sem.at[kind, o],
            device_id={"doc": peer},
            device_id_type=MESH,
        )

    def send(kind, o, src, dst):
        return send_any(kind, o, src, dst, peers[o])

    def cast(p, carry):
        bins_bf[p] = bins_ref[p].astype(F32).astype(BF)
        return carry

    bins_load.wait()
    lax.fori_loop(0, ndoc, cast, 0)
    pl.semaphore_wait(barrier, ndoc - 1)
    col_copies = [send(0, o, bins_bf.at[peers[o]], cols_ref.at[o]) for o in range(1, ndoc)]
    for copy in col_copies[:EARLY]:
        copy.start()
    cols_ref[0] = bins_bf[me]
    acc_ref[...] = jnp.zeros_like(acc_ref)

    for load in loads:
        load.wait()
    place = lax.broadcasted_iota(jnp.int32, (nq, npos), 1)
    shown = place < lengths_ref[...]
    clicked = jnp.logical_and(shown, clicks_ref[...] == 1)
    skipped = jnp.logical_and(shown, clicks_ref[...] == 0)
    code = jnp.where(clicked, 1.0, jnp.where(skipped, -1.0, 0.0)).astype(F32)
    count = jnp.sum(jnp.where(clicked, 1.0, 0.0), axis=1, keepdims=True)
    to_log2 = 1.4426950408889634
    disc_row = 1.0 / (jnp.log(2.0 + lax.broadcasted_iota(jnp.int32, (8, npos), 1).astype(F32)) * to_log2)
    disc_row = disc_row[0:1]
    ideal = jnp.sum(jnp.where(place.astype(F32) < count, disc_row, 0.0), axis=1, keepdims=True)
    gain = 1.0 / jnp.maximum(ideal, 1.0)
    weigh = jnp.where(clicked, 1.0 / tpo_ref[...], 1.0 / tmo_ref[...])
    turn[...] = jnp.zeros_like(turn)
    turn[0:nq] = scores_ref[...]
    turn[16 : 16 + nq] = code
    turn[32 : 32 + nq] = weigh
    turn[48:49] = disc_row
    stood = turn[...].T
    gap = jnp.abs(stood[:, 48:49] - disc_row)
    plus_row = jnp.zeros((1, npos), F32)
    minus_row = jnp.zeros((1, npos), F32)
    for q in range(nq):
        code_col = stood[:, 16 + q : 17 + q]
        code_row = code[q : q + 1]
        away = jnp.where(code_col * code_row < 0.0, gap, 0.0)
        y = code_col * (scores_ref[q : q + 1, :] - stood[:, q : q + 1])
        e = jnp.exp(-jnp.abs(y))
        inv = 1.0 / (1.0 + e)
        small = e * (1.0 - e * (0.5 - e * (1.0 / 3.0)))
        soft = jnp.maximum(y, 0.0) + jnp.where(e < 0.01, small, jnp.log(1.0 + e))
        loss = jnp.sum(away * soft * stood[:, 32 + q : 33 + q], axis=0, keepdims=True)
        loss = loss * gain[q : q + 1]
        plus_row = plus_row + jnp.where(code_row > 0.0, loss, 0.0)
        minus_row = minus_row + jnp.where(code_row < 0.0, loss, 0.0)
        scaled = away * inv
        pair_g[q] = code_col * scaled * jnp.where(y >= 0.0, 1.0, e)
        pair_h[q] = scaled * inv * e
    sums[me, 0:1] = plus_row
    sums[me, 1:2] = minus_row
    sum_copies = [send(1, o, sums.at[me], sums.at[me]) for o in range(1, ndoc)]
    for copy in sum_copies:
        copy.start()
    for copy in sum_copies:
        copy.wait()
    total = jnp.sum(sums[...], axis=0)
    t_new = jnp.sqrt(total / total[:, 0:1])
    tp_ref[...] = t_new[0:1]
    tm_ref[...] = t_new[1:2]
    t_inv = 1.0 / t_new
    unit = jnp.where(clicked, t_inv[0:1], t_inv[1:2])
    turn[0:nq] = unit
    unit_col = turn[...].T
    unit_row = unit * gain
    slopes, curves = [], []
    for q in range(nq):
        lanes = slice(q * npos, (q + 1) * npos)
        side = unit_col[:, q : q + 1]
        slope = jnp.sum(pair_g[q] * side, axis=0, keepdims=True) * unit_row[q : q + 1]
        curve = jnp.sum(pair_h[q] * side, axis=0, keepdims=True) * unit_row[q : q + 1]
        grad_ref[:, lanes] = jnp.concatenate([slope, curve], axis=0)
        slopes.append(slope)
        curves.append(curve)

    def largest(values):
        top = jnp.abs(values[0])
        for value in values[1:]:
            top = jnp.maximum(top, jnp.abs(value))
        return jnp.max(top, axis=1, keepdims=True)

    slope_up, slope_down = power_scale(largest(slopes), npos)
    curve_up, curve_down = power_scale(largest(curves), npos)
    for q in range(nq):
        lanes = slice(q * npos, (q + 1) * npos)
        leaf_row = leaf_ref[lanes].astype(F32).reshape(1, npos)
        down = slope_down if q < nq // 2 else curve_down
        pk_ref[0, :, lanes] = jnp.concatenate(
            [slopes[q] * slope_up, curves[q] * curve_up, leaf_row, down], axis=0
        ).astype(BF)
    pk_copies = [send(2, o, pk_ref.at[0], pk_ref.at[o]) for o in range(1, ndoc)]
    for copy in pk_copies:
        copy.start()
    for copy in col_copies[EARLY:]:
        copy.start()

    def add(o):
        add_block(lambda f: cols_ref[o, f : f + 1, :], pk_ref[o], acc_ref, w_ref)

    add(0)

    def arrived(o, carry):
        send_any(2, o, pk_ref.at[0], pk_ref.at[o]).wait_recv()
        send_any(0, o, bins_bf.at[0], cols_ref.at[o]).wait_recv()
        add(o)
        return carry

    lax.fori_loop(1, half, arrived, 0)
    for copy in pk_copies[half - 1 :] + col_copies[half - 1 :]:
        copy.wait_recv()
    for copy in pk_copies + col_copies:
        copy.wait_send()


def hist_kernel(
    cols_ref, pk_ref, acc_in, tp_in, tm_in, grad_in, out_ref, tp_ref, tm_ref, grad_ref, w_ref
):
    @pl.when(pl.program_id(0) == 0)
    def _():
        out_ref[...] = acc_in[...]
        tp_ref[...] = tp_in[...]
        tm_ref[...] = tm_in[...]
        grad_ref[...] = grad_in[...]

    add_block(lambda f: cols_ref[0, f : f + 1, :], pk_ref[0], out_ref, w_ref)


def body(scores, clicks, lengths, t_plus_old, t_minus_old, leaf, bins):
    ndoc = lax.axis_size("doc")
    nq, npos = scores.shape
    rows = leaf.shape[0]
    nfeat = bins.shape[0] // ndoc
    half = max(ndoc // 2, 1)
    anyw = pl.BlockSpec(memory_space=pltpu.HBM)
    vmem = pl.BlockSpec(memory_space=pltpu.VMEM)
    t_plus, t_minus, gradients, cols, packs, acc = pl.pallas_call(
        functools.partial(rows_kernel, ndoc),
        out_shape=(
            jax.ShapeDtypeStruct((1, npos), F32),
            jax.ShapeDtypeStruct((1, npos), F32),
            jax.ShapeDtypeStruct((2, rows), F32),
            jax.ShapeDtypeStruct((ndoc, nfeat, rows), BF),
            jax.ShapeDtypeStruct((ndoc, 4, rows), BF),
            jax.ShapeDtypeStruct((nfeat, 2 * LEAVES, BINS), F32),
        ),
        in_specs=[anyw, anyw, vmem, anyw, anyw, anyw, anyw],
        out_specs=(vmem,) * 6,
        scratch_shapes=[
            pltpu.VMEM((4 * LEAVES, rows), F8),
            pltpu.VMEM((ndoc, nfeat, rows), BF),
            pltpu.VMEM((ndoc, 2, npos), F32),
            pltpu.VMEM((npos, npos), F32),
            pltpu.VMEM((nq, npos, npos), F32),
            pltpu.VMEM((nq, npos, npos), F32),
            pltpu.VMEM((nq, npos), F32),
            pltpu.VMEM((nq, npos), jnp.int32),
            pltpu.VMEM((1, npos), F32),
            pltpu.VMEM((1, npos), F32),
            pltpu.VMEM((rows,), jnp.int32),
            pltpu.VMEM((ndoc, nfeat, rows), jnp.int32),
            pltpu.SemaphoreType.DMA((3, ndoc)),
            pltpu.SemaphoreType.DMA((3, ndoc)),
            pltpu.SemaphoreType.DMA((6,)),
        ],
        compiler_params=pltpu.CompilerParams(
            collective_id=0, has_side_effects=True, vmem_limit_bytes=40 << 20
        ),
    )(
        scores,
        clicks,
        lengths.reshape(nq, 1),
        t_plus_old.reshape(1, npos),
        t_minus_old.reshape(1, npos),
        leaf,
        bins.reshape(ndoc, nfeat, rows),
    )
    whole = [pl.BlockSpec(a.shape, lambda i: (0, 0)) for a in (t_plus, t_minus, gradients)]
    hist, t_plus, t_minus, gradients = pl.pallas_call(
        hist_kernel,
        grid=(ndoc - half,),
        out_shape=(
            jax.ShapeDtypeStruct((nfeat, 2 * LEAVES, BINS), F32),
            jax.ShapeDtypeStruct(t_plus.shape, F32),
            jax.ShapeDtypeStruct(t_minus.shape, F32),
            jax.ShapeDtypeStruct(gradients.shape, F32),
        ),
        in_specs=[
            pl.BlockSpec((1, nfeat, rows), lambda i: (i + half, 0, 0)),
            pl.BlockSpec((1, 4, rows), lambda i: (i + half, 0, 0)),
            pl.BlockSpec((nfeat, 2 * LEAVES, BINS), lambda i: (0, 0, 0)),
            *whole,
        ],
        out_specs=(pl.BlockSpec((nfeat, 2 * LEAVES, BINS), lambda i: (0, 0, 0)), *whole),
        scratch_shapes=[pltpu.VMEM((4 * LEAVES, rows), F8)],
        compiler_params=pltpu.CompilerParams(vmem_limit_bytes=40 << 20),
    )(cols, packs, acc, t_plus, t_minus, gradients)
    return (t_plus.reshape(npos), t_minus.reshape(npos), gradients, hist)


def solution(mesh):
    placed = (P("doc", None), P("doc", None), P("doc"), P(), P(), P("doc"), P("feat", "doc"))
    return jax.shard_map(
        body,
        mesh=mesh,
        in_specs=placed,
        out_specs=(P(), P(), P(None, "doc"), P(("feat", "doc"), None, None)),
        check_vma=False,
    )
```
